32 devices in a mesh: dom: 16 (over z, y, core), col: 2 (over x).
Axes of the slice: x: 2, y: 2, z: 4, core: 2. Of those that a mesh axis runs over, the one named last changes fastest.
Arguments:
- feats_t: bfloat16 [256, 32768], P('col', 'dom'), may hold values from -6 to 6
- weight: bfloat16 [256, 256], P('col'), may hold values from -0.375 to 0.375
- cotangent_t: bfloat16 [256, 32768], P('col', 'dom'), may hold values from -6 to 6
- tiles: bfloat16 [256, 8, 128, 128], P('dom'), may hold values from 0 to 0.1045825
- tile_cols: int32 [256, 8], P('dom'), may hold values from 0 to 79
- tile_count: int32 [256], P('dom'), may hold values from 5 to 8, as said below
- send_blocks: int32 [16, 8, 8], P('dom'), may hold values from 0 to 15, as said below
Outputs:
- output_t: bfloat16 [256, 32768], P('col', 'dom')
- grad_weight: float32 [256, 256], P('col')
- grad_feats_t: float32 [256, 32768], P('col', 'dom')
The draws below stay inside these ranges and needn't reach their ends.
Inputs may be any that keep to these rules, and one draw needn't show every extreme that they name: Slots from tile_count onward are padding and are not part of the adjacency. `send_blocks`: within one partition and round the 8 listed blocks are different.
All inputs are finite; a program needn't handle non-finite values.
Results may differ from the reference program's by a relative error of at most 0.0056.
Values may be sent and summed in bfloat16 or wider, within the bound.
A program may use at most 64 MiB of HBM per device.

```python
import jax
import jax.numpy as jnp
from jax import lax

DIN = 256
DOUT = 256
BLK = 128
NB = 16
ROUNDS = 8
TPR = 8
BB = 8
COVER = 5
NEXT = 80
PARTS_SIZE = 16
NBLK = 256
NODES = 32768


def draw_tiles(key, part):
    key = jax.random.fold_in(key, 10)
    base = jax.random.uniform(key, (NBLK, TPR, BLK, BLK), jnp.float32, 0.0, 1.0)
    level = (7.0 / (COVER * BLK)) ** 0.5
    values = level * base * base * base
    return values.astype(jnp.bfloat16)


def draw_tile_cols(key, part):
    key = jax.random.fold_in(key, 11)
    first_key, second_key = jax.random.split(key)
    part_keys = jax.random.split(first_key, PARTS_SIZE)
    orders = jax.vmap(lambda one_key: jax.random.permutation(one_key, NEXT))(part_keys)
    covered = orders.reshape(PARTS_SIZE * NB, COVER)
    extra = jax.random.randint(second_key, (PARTS_SIZE * NB, TPR - COVER), 0, NEXT)
    return jnp.concatenate([covered, extra], axis=1).astype(jnp.int32)


def draw_tile_count(key, part):
    key = jax.random.fold_in(key, 12)
    heavy_key, base_key, forced_key = jax.random.split(key, 3)
    heavy = jax.random.randint(heavy_key, (PARTS_SIZE, 1), 0, 4) == 0
    base = jax.random.randint(base_key, (PARTS_SIZE, NB), COVER, TPR + 1)
    forced = jax.random.randint(forced_key, (PARTS_SIZE, 1), 0, NB)
    position = jnp.arange(NB, dtype=jnp.int32)[None, :]
    counts = jnp.where(heavy | (position == forced), TPR, base)
    return counts.reshape(PARTS_SIZE * NB).astype(jnp.int32)


def draw_send_blocks(key, part):
    key = jax.random.fold_in(key, 13)
    round_keys = jax.random.split(key, PARTS_SIZE * ROUNDS)
    orders = jax.vmap(lambda one_key: jax.random.permutation(one_key, NB))(round_keys)
    return orders[:, :BB].reshape(PARTS_SIZE, ROUNDS, BB).astype(jnp.int32)


def steps_of(stream_key, shape, shards, least, high):
    def one(axis_at, parts):
        heights = jax.random.uniform(jax.random.fold_in(jax.random.fold_in(stream_key, 6), axis_at), (parts,), jnp.float32, least / len(shards), high / len(shards))
        return jnp.repeat(jnp.exp(heights), shape[axis_at] // parts).reshape((-1,) + (1,) * (len(shape) - axis_at - 1))

    gain = one(*shards[0])
    for cut in shards[1:]:
        gain = gain * one(*cut)
    return gain


def bell_draw(rng, dims, width, reach, cuts=(), kind=jnp.bfloat16):
    level = steps_of(rng, dims, cuts, -0.22, 0.18) if cuts else 1.0
    array = jax.random.normal(rng, dims, jnp.float32) * width * level
    return jnp.minimum(jnp.maximum(array, -reach), reach).astype(kind)


def setup_inputs(seed: int = 0) -> dict:
    keys = jax.random.split(jax.random.key(seed), 8)
    feats_t = bell_draw(keys[0], (DIN, NODES), 1.0, 6.0, ((0, 2), (1, 16)))
    weight = bell_draw(keys[1], (DIN, DOUT), DIN ** -0.5, 0.375, ((0, 2),))
    cotangent_t = bell_draw(keys[2], (DOUT, NODES), 1.0, 6.0, ((0, 2), (1, 16)))
    tiles = draw_tiles(jax.random.fold_in(keys[7], 71), 0)
    tile_cols = draw_tile_cols(jax.random.fold_in(keys[7], 71), 0)
    tile_count = draw_tile_count(jax.random.fold_in(keys[7], 71), 0)
    send_blocks = draw_send_blocks(jax.random.fold_in(keys[7], 71), 0)
    return {"feats_t": feats_t, "weight": weight, "cotangent_t": cotangent_t, "tiles": tiles, "tile_cols": tile_cols, "tile_count": tile_count, "send_blocks": send_blocks}


def round_offset(round_index):
    step_size = round_index // 2 + 1
    return step_size if round_index % 2 == 0 else -step_size


def silu_slope(values):
    sigma = jax.nn.sigmoid(values)
    return sigma * (1.0 + values * (1.0 - sigma))


def reference(feats_t, weight, cotangent_t, tiles, tile_cols, tile_count, send_blocks):
    own_blocks = feats_t.reshape(DIN, PARTS_SIZE, NB, BLK)
    tile_parts = tiles.reshape(PARTS_SIZE, NB, TPR, BLK, BLK)
    col_parts = tile_cols.reshape(PARTS_SIZE, NB, TPR)
    valid_parts = jnp.arange(TPR, dtype=jnp.int32)[None, None, :] < tile_count.reshape(PARTS_SIZE, NB)[:, :, None]
    highest = lax.Precision.HIGHEST

    def extended(part_index):
        pieces = [own_blocks[:, part_index]]
        for round_index in range(ROUNDS):
            source = ((part_index - round_offset(round_index)) % PARTS_SIZE).astype(jnp.int32)
            chosen = send_blocks[source, round_index]
            pieces.append(jnp.take(own_blocks[:, source], chosen, axis=1))
        return jnp.concatenate(pieces, axis=1)

    def forward_part(part_index):
        ext_rows = extended(part_index).astype(jnp.float32)
        picked = jnp.take(ext_rows, col_parts[part_index].reshape(-1), axis=1).reshape(DIN, NB, TPR, BLK)
        picked = jnp.where(valid_parts[part_index][None, :, :, None], picked, 0.0)
        summed = jnp.einsum('fbtc,btrc->fbr', picked, tile_parts[part_index].astype(jnp.float32), precision=highest)
        return summed.reshape(DIN, NB * BLK)

    parts_range = jnp.arange(PARTS_SIZE, dtype=jnp.int32)
    aggregated = lax.map(forward_part, parts_range)
    aggregated = aggregated.transpose(1, 0, 2).reshape(DIN, NODES).astype(jnp.bfloat16)
    pre_act = jnp.dot(weight.T, aggregated, preferred_element_type=jnp.float32)
    output_t = jax.nn.silu(pre_act).astype(jnp.bfloat16)
    grad_pre = (cotangent_t.astype(jnp.float32) * silu_slope(pre_act)).astype(jnp.bfloat16)
    grad_weight = jnp.dot(aggregated, grad_pre.T, preferred_element_type=jnp.float32)
    grad_agg = jnp.dot(weight, grad_pre, preferred_element_type=jnp.float32).astype(jnp.bfloat16)
    grad_blocks = grad_agg.reshape(DIN, PARTS_SIZE, NB, BLK)

    def backward_part(part_index):
        terms = jnp.einsum('fbr,btrc->fbtc', grad_blocks[:, part_index].astype(jnp.float32),
                           tile_parts[part_index].astype(jnp.float32), precision=highest)
        terms = jnp.where(valid_parts[part_index][None, :, :, None], terms, 0.0)
        empty = jnp.zeros((DIN, NEXT, BLK), jnp.float32)
        return empty.at[:, col_parts[part_index].reshape(-1)].add(terms.reshape(DIN, NB * TPR, BLK))

    ext_grad = lax.map(backward_part, parts_range)
    grad_own = ext_grad[:, :, :NB]
    for round_index in range(ROUNDS):
        piece = ext_grad[:, :, NB + round_index * BB:NB + (round_index + 1) * BB]
        back_rows = jnp.roll(piece, -round_offset(round_index), axis=0)
        grad_own = jax.vmap(lambda total, extra, index_list: total.at[:, index_list].add(extra))(
            grad_own, back_rows, send_blocks[:, round_index])
    grad_feats_t = grad_own.transpose(1, 0, 2, 3).reshape(DIN, NODES)
    return output_t, grad_weight, grad_feats_t
```

```python
import functools

import jax
import jax.numpy as jnp
from jax import lax
from jax.experimental import pallas as pl
from jax.experimental.pallas import tpu as pltpu
from jax.sharding import PartitionSpec as P

MESH = pl.DeviceIdType.MESH
CHUNKS = 4
BF = jnp.bfloat16
F32 = jnp.float32


def round_offset(round_index):
    step_size = round_index // 2 + 1
    return step_size if round_index % 2 == 0 else -step_size


def nt_dot(a, b):
    return lax.dot_general(a, b, (((1,), (1,)), ((), ())), preferred_element_type=F32)


def nn_dot(a, b):
    return lax.dot_general(a, b, (((1,), (0,)), ((), ())), preferred_element_type=F32)


def forward_kernel(
    cols, counts, lists, feats, cot_hbm, w_hbm, tiles_hbm,
    out_ref, gagg_ref, gw_ref,
    own, stage, ext, tiles, cot, w, wt, agg,
    z_send, z_recv, c_send, c_recv, w_send, w_recv, a_send, a_recv, local_sem,
):
    n_dom = lax.axis_size("dom")
    n_col = lax.axis_size("col")
    me = lax.axis_index("dom")
    c = lax.axis_index("col")
    rounds, per = lists.shape
    blocks, size = own.shape[0], own.shape[2]
    slots = tiles.shape[1]
    feat = own.shape[1]
    width = w.shape[0] * feat
    ext_total = blocks + rounds * per

    barrier = pltpu.get_barrier_semaphore()
    for r in range(rounds):
        target = lax.rem(me + round_offset(r) + n_dom, n_dom)
        pl.semaphore_signal(barrier, inc=1, device_id={"dom": target}, device_id_type=MESH)
    for d in range(1, n_col):
        target = lax.rem(c + d, n_col)
        pl.semaphore_signal(barrier, inc=1, device_id={"col": target}, device_id_type=MESH)

    load_tiles = pltpu.make_async_copy(tiles_hbm, tiles, local_sem.at[0])
    load_cot = pltpu.make_async_copy(cot_hbm, cot.at[c], local_sem.at[1])
    load_w = pltpu.make_async_copy(w_hbm, w.at[c], local_sem.at[2])
    load_w.start()
    load_cot.start()
    load_tiles.start()

    def split(b, carry):
        block = feats[:, pl.ds(pl.multiple_of(b * size, size), size)]
        own[b] = block
        ext[b] = block
        return carry

    lax.fori_loop(0, blocks, split, 0)
    ext[ext_total] = jnp.zeros((feat, size), BF)

    z_copies = []
    for r in range(rounds):
        target = lax.rem(me + round_offset(r) + n_dom, n_dom)
        for j in range(per):
            stage[r * per + j] = own[lists[r, j]]
        if r == 0:
            pl.semaphore_wait(barrier, rounds + n_col - 1)
        copy = pltpu.make_async_remote_copy(
            src_ref=stage.at[pl.ds(r * per, per)],
            dst_ref=ext.at[pl.ds(blocks + r * per, per)],
            send_sem=z_send.at[r], recv_sem=z_recv.at[r],
            device_id={"dom": target}, device_id_type=MESH,
        )
        copy.start()
        z_copies.append(copy)

    def col_copy(at, d, here, send_sem, recv_sem):
        return pltpu.make_async_remote_copy(
            src_ref=at(here), dst_ref=at(here), send_sem=send_sem, recv_sem=recv_sem,
            device_id={"col": lax.rem(c + d, n_col)}, device_id_type=MESH,
        )

    load_w.wait()
    for d in range(1, n_col):
        col_copy(lambda i: w.at[i], d, c, w_send.at[d - 1], w_recv.at[d - 1]).start()
    load_cot.wait()
    for d in range(1, n_col):
        col_copy(lambda i: cot.at[i], d, c, c_send.at[d - 1], c_recv.at[d - 1]).start()

    def col_wait(at, d, send_sem, recv_sem):
        there = lax.rem(c - d + n_col, n_col)
        col_copy(at, d, c, send_sem, recv_sem).wait_send()
        col_copy(at, d, there, send_sem, recv_sem).wait_recv()

    for d in range(1, n_col):
        col_wait(lambda i: w.at[i], d, w_send.at[d - 1], w_recv.at[d - 1])
    turned = w[...].reshape(width, -1).astype(F32).T.astype(BF)
    wt[...] = turned.reshape(wt.shape)

    load_tiles.wait()
    for copy in z_copies:
        copy.wait()

    step = blocks // CHUNKS
    span = step * size
    for i in range(CHUNKS):
        def one(k, carry):
            b = i * step + k
            count = counts[b]
            picked = jnp.concatenate(
                [ext[jnp.where(t < count, cols[b, t], ext_total)] for t in range(slots)], axis=1
            )
            rows = jnp.concatenate([tiles[b, t] for t in range(slots)], axis=1)
            total = nt_dot(picked, rows).astype(BF)
            agg[i, c, :, pl.ds(pl.multiple_of(k * size, size), size)] = total
            return carry

        lax.fori_loop(0, step, one, 0)
        for d in range(1, n_col):
            col_copy(lambda q: agg.at[i, q], d, c, a_send.at[i, d - 1], a_recv.at[i, d - 1]).start()

    for d in range(1, n_col):
        col_wait(lambda q: cot.at[q], d, c_send.at[d - 1], c_recv.at[d - 1])

    gw = jnp.zeros((feat, width), F32)
    for i in range(CHUNKS):
        for d in range(1, n_col):
            col_wait(lambda q: agg.at[i, q], d, a_send.at[i, d - 1], a_recv.at[i, d - 1])
        whole = agg[i].reshape(width, span)
        pre = nn_dot(wt[...].reshape(width, width), whole)
        sigma = jax.nn.sigmoid(pre)
        slope = sigma * (1.0 + pre * (1.0 - sigma))
        held = cot[:, :, i * span : (i + 1) * span].reshape(width, span).astype(F32)
        grad = (held * slope).astype(BF)
        mine = nn_dot(wt[c], whole)
        out_ref[:, i * span : (i + 1) * span] = (mine * jax.nn.sigmoid(mine)).astype(BF)
        back = nn_dot(w[c], grad).astype(BF)
        for k in range(step):
            gagg_ref[i * step + k] = back[:, k * size : (k + 1) * size]
        gw = gw + nt_dot(agg[i, c], grad)
    half = gw_ref.shape[1]
    for h in range(width // half):
        gw_ref[h * feat : (h + 1) * feat] = gw[:, h * half : (h + 1) * half]


def scatter_kernel(cols, counts, gagg, tiles, own_ref, ext_ref, acc):
    step = pl.program_id(0)
    per_step, slots = tiles.shape[0], tiles.shape[1]
    blocks = own_ref.shape[0]
    total = acc.shape[0] - 1

    @pl.when(step == 0)
    def _():
        acc[...] = jnp.zeros_like(acc)

    for k in range(per_step):
        b = step * per_step + k
        count = counts[b]
        grad = gagg[k]
        for t in range(slots):
            at = jnp.where(t < count, cols[b, t], total)
            acc[at] += nn_dot(grad, tiles[k, t])

    @pl.when(step == pl.num_programs(0) - 1)
    def _():
        own_ref[...] = acc[:blocks]
        ext_ref[...] = acc[blocks:total].astype(BF)


def return_kernel(
    reduce_here, lists, ext_hbm, own, gw,
    out_ref, gw_out,
    got0, got1, got2, got3, got4, got5, got6, got7, parts, sums,
    z_send, z_recv, p_send, p_recv, s_send, s_recv, local_sem,
):
    got = [got0, got1, got2, got3, got4, got5, got6, got7]
    n_dom = lax.axis_size("dom")
    me = lax.axis_index("dom")
    rounds, per = lists.shape
    blocks, feat, size = own.shape

    def peer(distance):
        return lax.rem(me + distance + n_dom, n_dom)

    barrier = pltpu.get_barrier_semaphore()
    if reduce_here:
        def greet(d, carry):
            pl.semaphore_signal(barrier, inc=1, device_id={"dom": peer(d)}, device_id_type=MESH)
            return carry

        lax.fori_loop(1, n_dom, greet, 0)
    else:
        for r in range(rounds):
            pl.semaphore_signal(
                barrier, inc=1, device_id={"dom": peer(round_offset(r))}, device_id_type=MESH
            )
    for r in range(rounds):
        got[r][per] = jnp.zeros((feat, size), BF)
    pl.semaphore_wait(barrier, n_dom - 1 if reduce_here else rounds)

    def part_copy(d, target_slot, source_slot):
        return pltpu.make_async_remote_copy(
            src_ref=gw.at[source_slot], dst_ref=parts.at[target_slot],
            send_sem=p_send.at[d], recv_sem=p_recv.at[d],
            device_id={"dom": peer(d)}, device_id_type=MESH,
        )

    def sum_copy(d, slot):
        return pltpu.make_async_remote_copy(
            src_ref=sums.at[slot], dst_ref=sums.at[slot],
            send_sem=s_send.at[d], recv_sem=s_recv.at[d],
            device_id={"dom": peer(d)}, device_id_type=MESH,
        )

    if reduce_here:
        def send_part(d, carry):
            part_copy(d, d, peer(d)).start()
            return carry

        lax.fori_loop(1, n_dom, send_part, 0)

    copies = []
    for r in range(rounds):
        copy = pltpu.make_async_remote_copy(
            src_ref=ext_hbm.at[pl.ds(r * per, per)],
            dst_ref=got[r].at[pl.ds(0, per)],
            send_sem=z_send.at[r], recv_sem=z_recv.at[r],
            device_id={"dom": peer(-round_offset(r))}, device_id_type=MESH,
        )
        copy.start()
        copies.append(copy)

    if reduce_here:
        def wait_part(d, total):
            part_copy(d, d, peer(d)).wait()
            return total + parts[d]

        sums[me] = lax.fori_loop(1, n_dom, wait_part, gw[me])

        def send_sum(d, carry):
            sum_copy(d, me).start()
            return carry

        lax.fori_loop(1, n_dom, send_sum, 0)

    for r in range(rounds):
        copies[r].wait()

        def add(b, carry):
            at = per
            for j in range(per):
                at = jnp.where(lists[r, j] == b, j, at)
            columns = pl.ds(pl.multiple_of(b * size, size), size)
            base = own[b] if r == 0 else out_ref[:, columns]
            out_ref[:, columns] = base + got[r][at].astype(F32)
            return carry

        lax.fori_loop(0, blocks, add, 0)

    if reduce_here:
        def wait_sum(d, carry):
            sum_copy(d, me).wait_send()
            sum_copy(d, peer(-d)).wait_recv()
            return carry

        lax.fori_loop(1, n_dom, wait_sum, 0)
        flat = sums[...].reshape(-1, sums.shape[2])
        feat_rows = gw_out.shape[0]
        half = sums.shape[2]
        for h in range(gw_out.shape[1] // half):
            gw_out[:, h * half : (h + 1) * half] = flat[h * feat_rows : (h + 1) * feat_rows]
    else:
        gw_out[...] = jnp.zeros_like(gw_out)


def shards(n_dom, n_col, feats_t, weight, cotangent_t, tiles, tile_cols, tile_count, send_blocks):
    feat, nodes = feats_t.shape
    width = feat * n_col
    blocks, slots, size, _ = tiles.shape
    rounds, per = send_blocks.shape[1:]
    extra = rounds * per
    lists = send_blocks[0]
    step = blocks // CHUNKS
    span = step * size
    vmem = pl.BlockSpec(memory_space=pltpu.VMEM)
    smem = pl.BlockSpec(memory_space=pltpu.SMEM)
    anywhere = pl.BlockSpec(memory_space=pl.ANY)
    dma = pltpu.SemaphoreType.DMA
    half = 128

    output_t, gagg, gw = pl.pallas_call(
        forward_kernel,
        out_shape=(
            jax.ShapeDtypeStruct((feat, nodes), BF),
            jax.ShapeDtypeStruct((blocks, feat, size), BF),
            jax.ShapeDtypeStruct((feat * (width // half), half), F32),
        ),
        in_specs=[smem, smem, smem, vmem, anywhere, anywhere, anywhere],
        out_specs=(vmem, vmem, vmem),
        scratch_shapes=[
            pltpu.VMEM((blocks, feat, size), BF),
            pltpu.VMEM((extra, feat, size), BF),
            pltpu.VMEM((blocks + extra + 1, feat, size), BF),
            pltpu.VMEM(tiles.shape, BF),
            pltpu.VMEM((n_col, feat, nodes), BF),
            pltpu.VMEM((n_col, feat, width), BF),
            pltpu.VMEM((n_col, feat, width), BF),
            pltpu.VMEM((CHUNKS, n_col, feat, span), BF),
            dma((rounds,)), dma((rounds,)),
            dma((n_col - 1,)), dma((n_col - 1,)),
            dma((n_col - 1,)), dma((n_col - 1,)),
            dma((CHUNKS, n_col - 1)), dma((CHUNKS, n_col - 1)),
            dma((3,)),
        ],
        compiler_params=pltpu.CompilerParams(
            collective_id=0, has_side_effects=True, vmem_limit_bytes=40 * 2**20
        ),
        name="forward",
    )(tile_cols, tile_count, lists, feats_t, cotangent_t, weight, tiles)

    per_step = blocks // CHUNKS
    own, ext = pl.pallas_call(
        scatter_kernel,
        grid=(CHUNKS,),
        out_shape=(
            jax.ShapeDtypeStruct((blocks, feat, size), F32),
            jax.ShapeDtypeStruct((extra, feat, size), BF),
        ),
        in_specs=[
            smem, smem,
            pl.BlockSpec((per_step, feat, size), lambda i: (i, 0, 0)),
            pl.BlockSpec((per_step, slots, size, size), lambda i: (i, 0, 0, 0)),
        ],
        out_specs=(
            pl.BlockSpec((blocks, feat, size), lambda i: (0, 0, 0)),
            pl.BlockSpec((extra, feat, size), lambda i: (0, 0, 0)),
        ),
        scratch_shapes=[pltpu.VMEM((blocks + extra + 1, feat, size), F32)],
        compiler_params=pltpu.CompilerParams(vmem_limit_bytes=32 * 2**20),
        name="scatter",
    )(tile_cols, tile_count, gagg, tiles)

    total_rows = feat * (width // half)
    reduce_here = total_rows % n_dom == 0 and (total_rows // n_dom) % 8 == 0
    rows = total_rows // n_dom if reduce_here else 8
    parts_n = n_dom if reduce_here else 1
    gw_in = gw.reshape(n_dom, rows, half) if reduce_here else jnp.zeros((1, 8, half), F32)
    grad_feats_t, grad_weight = pl.pallas_call(
        functools.partial(return_kernel, reduce_here),
        out_shape=(
            jax.ShapeDtypeStruct((feat, nodes), F32),
            jax.ShapeDtypeStruct((feat, width), F32),
        ),
        in_specs=[smem, anywhere, vmem, vmem],
        out_specs=(vmem, vmem),
        scratch_shapes=[pltpu.VMEM((per + 1, feat, size), BF)] * rounds
        + [
            pltpu.VMEM((parts_n, rows, half), F32),
            pltpu.VMEM((parts_n, rows, half), F32),
            dma((rounds,)), dma((rounds,)),
            dma((n_dom,)), dma((n_dom,)),
            dma((n_dom,)), dma((n_dom,)),
            dma((1,)),
        ],
        compiler_params=pltpu.CompilerParams(
            collective_id=1, has_side_effects=True, vmem_limit_bytes=24 * 2**20
        ),
        name="give_back",
    )(lists, ext, own, gw_in)
    if not reduce_here:
        summed = lax.psum(gw, "dom").reshape(width // half, feat, half)
        grad_weight = summed.transpose(1, 0, 2).reshape(feat, width)
    return (output_t, grad_weight, grad_feats_t)


def solution(mesh):
    placed = (
        P("col", "dom"),
        P("col", None),
        P("col", "dom"),
        P("dom", None, None, None),
        P("dom", None),
        P("dom"),
        P("dom", None, None),
    )
    return jax.shard_map(
        functools.partial(shards, mesh.shape["dom"], mesh.shape["col"]),
        mesh=mesh,
        in_specs=placed,
        out_specs=(P("col", "dom"), P("col", None), P("col", "dom")),
        check_vma=False,
    )
```

```python
import functools

import jax
import jax.numpy as jnp
from jax import lax
from jax.experimental import pallas as pl
from jax.experimental.pallas import tpu as pltpu
from jax.sharding import PartitionSpec as P

MESH = pl.DeviceIdType.MESH
CHUNKS = 4
LANES = 4
BF = jnp.bfloat16
F32 = jnp.float32


def round_offset(round_index):
    step_size = round_index // 2 + 1
    return step_size if round_index % 2 == 0 else -step_size


def nt_dot(a, b):
    return lax.dot_general(a, b, (((1,), (1,)), ((), ())), preferred_element_type=F32)


def nn_dot(a, b):
    return lax.dot_general(a, b, (((1,), (0,)), ((), ())), preferred_element_type=F32)


def forward_kernel(
    cols, counts, lists, feats, cot_hbm, w_hbm, tiles_hbm,
    out_ref, gagg_ref, gw_ref,
    own, stage, ext0, ext1, tiles, cot, w, wt, agg,
    z_send, z_recv, c_send, c_recv, w_send, w_recv, a_send, a_recv, local_sem,
):
    n_dom = lax.axis_size("dom")
    n_col = lax.axis_size("col")
    me = lax.axis_index("dom")
    c = lax.axis_index("col")
    rounds, per = lists.shape
    blocks, size = own.shape[0], own.shape[2]
    slots = tiles.shape[1]
    feat = own.shape[1]
    width = w.shape[0] * feat
    ext_total = blocks + rounds * per
    part = feat // 2
    exts = [ext0, ext1]

    barrier = pltpu.get_barrier_semaphore()
    for r in range(rounds):
        target = lax.rem(me + round_offset(r) + n_dom, n_dom)
        pl.semaphore_signal(barrier, inc=1, device_id={"dom": target}, device_id_type=MESH)
    for d in range(1, n_col):
        target = lax.rem(c + d, n_col)
        pl.semaphore_signal(barrier, inc=1, device_id={"col": target}, device_id_type=MESH)

    load_tiles = pltpu.make_async_copy(tiles_hbm, tiles, local_sem.at[0])
    load_cot = pltpu.make_async_copy(cot_hbm, cot.at[c], local_sem.at[1])
    load_w = pltpu.make_async_copy(w_hbm, w.at[c], local_sem.at[2])
    load_w.start()
    load_cot.start()
    load_tiles.start()

    def split(b, carry):
        block = feats[:, pl.ds(pl.multiple_of(b * size, size), size)]
        own[b] = block
        ext0[b] = block[:part]
        ext1[b] = block[part:]
        return carry

    lax.fori_loop(0, blocks, split, 0)
    ext0[ext_total] = jnp.zeros((part, size), BF)
    ext1[ext_total] = jnp.zeros((part, size), BF)

    def z_copy(h, r):
        target = lax.rem(me + round_offset(r) + n_dom, n_dom)
        return pltpu.make_async_remote_copy(
            src_ref=stage.at[h, pl.ds(r * per, per)],
            dst_ref=exts[h].at[pl.ds(blocks + r * per, per)],
            send_sem=z_send.at[h, r], recv_sem=z_recv.at[h, r],
            device_id={"dom": target}, device_id_type=MESH,
        )

    order = list(range(rounds))
    for r in order:
        for j in range(per):
            block = own[lists[r, j]]
            stage[0, r * per + j] = block[:part]
            stage[1, r * per + j] = block[part:]
        if r == order[0]:
            pl.semaphore_wait(barrier, rounds + n_col - 1)
        z_copy(0, r).start()

    def col_copy(at, d, here, send_sem, recv_sem):
        return pltpu.make_async_remote_copy(
            src_ref=at(here), dst_ref=at(here), send_sem=send_sem, recv_sem=recv_sem,
            device_id={"col": lax.rem(c + d, n_col)}, device_id_type=MESH,
        )

    load_w.wait()
    for d in range(1, n_col):
        col_copy(lambda i: w.at[i], d, c, w_send.at[d - 1], w_recv.at[d - 1]).start()
    load_cot.wait()
    for d in range(1, n_col):
        col_copy(lambda i: cot.at[i], d, c, c_send.at[d - 1], c_recv.at[d - 1]).start()

    def col_wait(at, d, send_sem, recv_sem):
        there = lax.rem(c - d + n_col, n_col)
        col_copy(at, d, c, send_sem, recv_sem).wait_send()
        col_copy(at, d, there, send_sem, recv_sem).wait_recv()

    for d in range(1, n_col):
        col_wait(lambda i: w.at[i], d, w_send.at[d - 1], w_recv.at[d - 1])
    turned = w[...].reshape(width, -1).astype(F32).T.astype(BF)
    wt[...] = turned.reshape(wt.shape)

    for r in order:
        z_copy(0, r).wait_send()
        z_copy(1, r).start()
    load_tiles.wait()

    step = blocks // CHUNKS
    span = step * size

    def agg_part(i, h):
        return lambda q: agg.at[i, q, pl.ds(h * part, part)]

    for h in range(2):
        ext = exts[h]
        for r in order:
            z_copy(h, r).wait_recv()
            if h == 1:
                z_copy(h, r).wait_send()
        for i in range(CHUNKS):
            def one(k, carry):
                b = i * step + k
                count = counts[b]
                picked = jnp.concatenate(
                    [ext[jnp.where(t < count, cols[b, t], ext_total)] for t in range(slots)], axis=1
                )
                rows = jnp.concatenate([tiles[b, t] for t in range(slots)], axis=1)
                total = nt_dot(picked, rows).astype(BF)
                columns = pl.ds(pl.multiple_of(k * size, size), size)
                agg[i, c, h * part : (h + 1) * part, columns] = total
                return carry

            lax.fori_loop(0, step, one, 0)
            for d in range(1, n_col):
                col_copy(
                    agg_part(i, h), d, c, a_send.at[h, i, d - 1], a_recv.at[h, i, d - 1]
                ).start()

    for d in range(1, n_col):
        col_wait(lambda q: cot.at[q], d, c_send.at[d - 1], c_recv.at[d - 1])

    gw = jnp.zeros((feat, width), F32)
    for i in range(CHUNKS):
        for d in range(1, n_col):
            for h in range(2):
                col_wait(agg_part(i, h), d, a_send.at[h, i, d - 1], a_recv.at[h, i, d - 1])
        whole = agg[i].reshape(width, span)
        pre = nn_dot(wt[...].reshape(width, width), whole)
        sigma = jax.nn.sigmoid(pre)
        slope = sigma * (1.0 + pre * (1.0 - sigma))
        held = cot[:, :, i * span : (i + 1) * span].reshape(width, span).astype(F32)
        grad = (held * slope).astype(BF)
        mine = nn_dot(wt[c], whole)
        out_ref[:, i * span : (i + 1) * span] = (mine * jax.nn.sigmoid(mine)).astype(BF)
        back = nn_dot(w[c], grad).astype(BF)
        for k in range(step):
            gagg_ref[i * step + k] = back[:, k * size : (k + 1) * size]
        gw = gw + nt_dot(agg[i, c], grad)
    half = gw_ref.shape[1]
    for h in range(width // half):
        gw_ref[h * feat : (h + 1) * feat] = gw[:, h * half : (h + 1) * half]


def scatter_kernel(cols, counts, gagg, tiles, own_ref, ext_ref, acc):
    step = pl.program_id(0)
    per_step, slots = tiles.shape[0], tiles.shape[1]
    blocks = own_ref.shape[0]
    total = acc.shape[0] - 1

    @pl.when(step == 0)
    def _():
        acc[...] = jnp.zeros_like(acc)

    for k in range(per_step):
        b = step * per_step + k
        count = counts[b]
        grad = gagg[k]
        for t in range(slots):
            at = jnp.where(t < count, cols[b, t], total)
            acc[at] += nn_dot(grad, tiles[k, t])

    @pl.when(step == pl.num_programs(0) - 1)
    def _():
        own_ref[...] = acc[:blocks]
        ext_ref[...] = acc[blocks:total].astype(BF)


def return_kernel(
    reduce_here, lists, ext_hbm, own, gw,
    out_ref, gw_out,
    got0, got1, got2, got3, got4, got5, got6, got7, lane_in, lane_sum, layer_in, sums,
    z_send, z_recv, a0, a1, b0, b1, c0, c1, d0, d1,
):
    sem_a, sem_b, sem_c, sem_d = (a0, a1), (b0, b1), (c0, c1), (d0, d1)
    got = [got0, got1, got2, got3, got4, got5, got6, got7]
    n_dom = lax.axis_size("dom")
    me = lax.axis_index("dom")
    rounds, per = lists.shape
    blocks, feat, size = own.shape

    def peer(distance):
        return lax.rem(me + distance + n_dom, n_dom)

    layers = n_dom // LANES
    layer = me // LANES
    lane = lax.rem(me, LANES)
    near = {round_offset(r) % n_dom for r in range(rounds)}
    if reduce_here:
        near |= {d * LANES for d in range(1, layers)}
        near |= {d % n_dom for d in range(1 - LANES, LANES) if d}
    near = sorted(near)
    barrier = pltpu.get_barrier_semaphore()
    for d in near:
        pl.semaphore_signal(barrier, inc=1, device_id={"dom": peer(d)}, device_id_type=MESH)
    for r in range(rounds):
        got[r][per] = jnp.zeros((feat, size), BF)
    pl.semaphore_wait(barrier, len(near))

    def lane_at(j):
        return lax.rem(lane + j + LANES, LANES)

    def layer_at(j):
        return lax.rem(layer + j + layers, layers)

    def dom_copy(src, dst, sems, j, target):
        return pltpu.make_async_remote_copy(
            src_ref=src, dst_ref=dst, send_sem=sems[0].at[j], recv_sem=sems[1].at[j],
            device_id={"dom": target}, device_id_type=MESH,
        )

    def lane_device(j):
        return layer * LANES + lane_at(j)

    def layer_device(j):
        return layer_at(j) * LANES + lane

    def first(j):
        return dom_copy(gw.at[lane_at(j)], lane_in.at[j], sem_a, j, lane_device(j))

    def second(j):
        return dom_copy(lane_sum.at[layer_at(j)], layer_in.at[j], sem_b, j, layer_device(j))

    def third(j, at):
        return dom_copy(sums.at[lane, at], sums.at[lane, at], sem_c, j, layer_device(j))

    def fourth(j, at):
        return dom_copy(sums.at[at], sums.at[at], sem_d, j, lane_device(j))

    def stage_one():
        for j in range(1, LANES):
            first(j).start()

    def stage_two():
        total = gw[lane]
        for j in range(1, LANES):
            first(j).wait()
            total = total + lane_in[j]
        lane_sum[...] = total
        for j in range(1, layers):
            second(j).start()

    def stage_three():
        total = lane_sum[layer]
        for j in range(1, layers):
            second(j).wait()
            total = total + layer_in[j]
        sums[lane, layer] = total
        for j in range(1, layers):
            third(j, layer).start()

    def stage_four():
        for j in range(1, layers):
            third(j, layer).wait_send()
            third(j, layer_at(-j)).wait_recv()
        for j in range(1, LANES):
            fourth(j, lane).start()

    stages = {0: stage_two, 2: stage_three, 4: stage_four} if reduce_here else {}
    if reduce_here:
        stage_one()

    copies = []
    for r in range(rounds):
        copy = pltpu.make_async_remote_copy(
            src_ref=ext_hbm.at[pl.ds(r * per, per)],
            dst_ref=got[r].at[pl.ds(0, per)],
            send_sem=z_send.at[r], recv_sem=z_recv.at[r],
            device_id={"dom": peer(-round_offset(r))}, device_id_type=MESH,
        )
        copy.start()
        copies.append(copy)

    for r in range(rounds):
        if r in stages:
            stages[r]()
        copies[r].wait()

        def add(b, carry):
            at = per
            for j in range(per):
                at = jnp.where(lists[r, j] == b, j, at)
            columns = pl.ds(pl.multiple_of(b * size, size), size)
            base = own[b] if r == 0 else out_ref[:, columns]
            out_ref[:, columns] = base + got[r][at].astype(F32)
            return carry

        lax.fori_loop(0, blocks, add, 0)

    if reduce_here:
        for j in range(1, LANES):
            fourth(j, lane).wait_send()
            fourth(j, lane_at(-j)).wait_recv()
        half = sums.shape[3]
        flat = sums[...].reshape(-1, half)
        feat_rows = gw_out.shape[0]
        for h in range(gw_out.shape[1] // half):
            gw_out[:, h * half : (h + 1) * half] = flat[h * feat_rows : (h + 1) * feat_rows]
    else:
        gw_out[...] = jnp.zeros_like(gw_out)


def shards(n_dom, n_col, feats_t, weight, cotangent_t, tiles, tile_cols, tile_count, send_blocks):
    feat, nodes = feats_t.shape
    width = feat * n_col
    blocks, slots, size, _ = tiles.shape
    rounds, per = send_blocks.shape[1:]
    extra = rounds * per
    lists = send_blocks[0]
    step = blocks // CHUNKS
    span = step * size
    vmem = pl.BlockSpec(memory_space=pltpu.VMEM)
    smem = pl.BlockSpec(memory_space=pltpu.SMEM)
    anywhere = pl.BlockSpec(memory_space=pl.ANY)
    dma = pltpu.SemaphoreType.DMA
    half = 128

    output_t, gagg, gw = pl.pallas_call(
        forward_kernel,
        out_shape=(
            jax.ShapeDtypeStruct((feat, nodes), BF),
            jax.ShapeDtypeStruct((blocks, feat, size), BF),
            jax.ShapeDtypeStruct((feat * (width // half), half), F32),
        ),
        in_specs=[smem, smem, smem, vmem, anywhere, anywhere, anywhere],
        out_specs=(vmem, vmem, vmem),
        scratch_shapes=[
            pltpu.VMEM((blocks, feat, size), BF),
            pltpu.VMEM((2, extra, feat // 2, size), BF),
            pltpu.VMEM((blocks + extra + 1, feat // 2, size), BF),
            pltpu.VMEM((blocks + extra + 1, feat // 2, size), BF),
            pltpu.VMEM(tiles.shape, BF),
            pltpu.VMEM((n_col, feat, nodes), BF),
            pltpu.VMEM((n_col, feat, width), BF),
            pltpu.VMEM((n_col, feat, width), BF),
            pltpu.VMEM((CHUNKS, n_col, feat, span), BF),
            dma((2, rounds)), dma((2, rounds)),
            dma((n_col - 1,)), dma((n_col - 1,)),
            dma((n_col - 1,)), dma((n_col - 1,)),
            dma((2, CHUNKS, n_col - 1)), dma((2, CHUNKS, n_col - 1)),
            dma((3,)),
        ],
        compiler_params=pltpu.CompilerParams(
            collective_id=0, has_side_effects=True, vmem_limit_bytes=60 * 2**20
        ),
        name="forward",
    )(tile_cols, tile_count, lists, feats_t, cotangent_t, weight, tiles)

    per_step = blocks // CHUNKS
    own, ext = pl.pallas_call(
        scatter_kernel,
        grid=(CHUNKS,),
        out_shape=(
            jax.ShapeDtypeStruct((blocks, feat, size), F32),
            jax.ShapeDtypeStruct((extra, feat, size), BF),
        ),
        in_specs=[
            smem, smem,
            pl.BlockSpec((per_step, feat, size), lambda i: (i, 0, 0)),
            pl.BlockSpec((per_step, slots, size, size), lambda i: (i, 0, 0, 0)),
        ],
        out_specs=(
            pl.BlockSpec((blocks, feat, size), lambda i: (0, 0, 0)),
            pl.BlockSpec((extra, feat, size), lambda i: (0, 0, 0)),
        ),
        scratch_shapes=[pltpu.VMEM((blocks + extra + 1, feat, size), F32)],
        compiler_params=pltpu.CompilerParams(vmem_limit_bytes=60 * 2**20),
        name="scatter",
    )(tile_cols, tile_count, gagg, tiles)

    total_rows = feat * (width // half)
    reduce_here = n_dom % LANES == 0 and total_rows % n_dom == 0 and (total_rows // n_dom) % 8 == 0
    rows = total_rows // n_dom if reduce_here else 8
    layers = n_dom // LANES if reduce_here else 1
    gw_in = gw if reduce_here else jnp.zeros((LANES * rows, half), F32)
    gw_in = gw_in.reshape(LANES, layers, rows, half)
    grad_feats_t, grad_weight = pl.pallas_call(
        functools.partial(return_kernel, reduce_here),
        out_shape=(
            jax.ShapeDtypeStruct((feat, nodes), F32),
            jax.ShapeDtypeStruct((feat, width), F32),
        ),
        in_specs=[smem, anywhere, vmem, vmem],
        out_specs=(vmem, vmem),
        scratch_shapes=[pltpu.VMEM((per + 1, feat, size), BF)] * rounds
        + [
            pltpu.VMEM((LANES, layers, rows, half), F32),
            pltpu.VMEM((layers, rows, half), F32),
            pltpu.VMEM((layers, rows, half), F32),
            pltpu.VMEM((LANES, layers, rows, half), F32),
            dma((rounds,)), dma((rounds,)),
            dma((LANES,)), dma((LANES,)),
            dma((layers,)), dma((layers,)),
            dma((layers,)), dma((layers,)),
            dma((LANES,)), dma((LANES,)),
        ],
        compiler_params=pltpu.CompilerParams(
            collective_id=1, has_side_effects=True, vmem_limit_bytes=48 * 2**20
        ),
        name="give_back",
    )(lists, ext, own, gw_in)
    if not reduce_here:
        summed = lax.psum(gw, "dom").reshape(width // half, feat, half)
        grad_weight = summed.transpose(1, 0, 2).reshape(feat, width)
    return (output_t, grad_weight, grad_feats_t)


def solution(mesh):
    placed = (
        P("col", "dom"),
        P("col", None),
        P("col", "dom"),
        P("dom", None, None, None),
        P("dom", None),
        P("dom"),
        P("dom", None, None),
    )
    return jax.shard_map(
        functools.partial(shards, mesh.shape["dom"], mesh.shape["col"]),
        mesh=mesh,
        in_specs=placed,
        out_specs=(P("col", "dom"), P("col", None), P("col", "dom")),
        check_vma=False,
    )
```

```python
import functools

import jax
import jax.numpy as jnp
from jax import lax
from jax.experimental import pallas as pl
from jax.experimental.pallas import tpu as pltpu
from jax.sharding import PartitionSpec as P

MESH = pl.DeviceIdType.MESH
CHUNKS = 4
LANES = 4
BF = jnp.bfloat16
F32 = jnp.float32


def round_offset(round_index):
    step_size = round_index // 2 + 1
    return step_size if round_index % 2 == 0 else -step_size


def farthest_first(rounds):
    return sorted(range(rounds), key=lambda r: -abs(round_offset(r)))


def nt_dot(a, b):
    return lax.dot_general(a, b, (((1,), (1,)), ((), ())), preferred_element_type=F32)


def nn_dot(a, b):
    return lax.dot_general(a, b, (((1,), (0,)), ((), ())), preferred_element_type=F32)


def forward_kernel(
    cols, counts, lists, feats, cot_hbm, w_hbm, tiles_hbm,
    out_ref, gagg_ref, gw_ref,
    own, stage, ext0, ext1, tiles, cot, w, wt, agg,
    z_send, z_recv, c_send, c_recv, w_send, w_recv, a_send, a_recv, local_sem,
):
    n_dom = lax.axis_size("dom")
    n_col = lax.axis_size("col")
    me = lax.axis_index("dom")
    c = lax.axis_index("col")
    rounds, per = lists.shape
    blocks, size = own.shape[0], own.shape[2]
    slots = tiles.shape[1]
    feat = own.shape[1]
    width = w.shape[0] * feat
    ext_total = blocks + rounds * per
    part = feat // 2
    exts = [ext0, ext1]

    barrier = pltpu.get_barrier_semaphore()
    for r in range(rounds):
        target = lax.rem(me + round_offset(r) + n_dom, n_dom)
        pl.semaphore_signal(barrier, inc=1, device_id={"dom": target}, device_id_type=MESH)
    for d in range(1, n_col):
        target = lax.rem(c + d, n_col)
        pl.semaphore_signal(barrier, inc=1, device_id={"col": target}, device_id_type=MESH)

    load_tiles = pltpu.make_async_copy(tiles_hbm, tiles, local_sem.at[0])
    load_cot = pltpu.make_async_copy(cot_hbm, cot.at[c], local_sem.at[1])
    load_w = pltpu.make_async_copy(w_hbm, w.at[c], local_sem.at[2])
    load_w.start()
    load_cot.start()
    load_tiles.start()

    def split(b, carry):
        block = feats[:, pl.ds(pl.multiple_of(b * size, size), size)]
        own[b] = block
        ext0[b] = block[:part]
        ext1[b] = block[part:]
        return carry

    lax.fori_loop(0, blocks, split, 0)
    ext0[ext_total] = jnp.zeros((part, size), BF)
    ext1[ext_total] = jnp.zeros((part, size), BF)

    def z_copy(h, r):
        target = lax.rem(me + round_offset(r) + n_dom, n_dom)
        return pltpu.make_async_remote_copy(
            src_ref=stage.at[h, pl.ds(r * per, per)],
            dst_ref=exts[h].at[pl.ds(blocks + r * per, per)],
            send_sem=z_send.at[h, r], recv_sem=z_recv.at[h, r],
            device_id={"dom": target}, device_id_type=MESH,
        )

    order = farthest_first(rounds)
    for r in order:
        for j in range(per):
            block = own[lists[r, j]]
            stage[0, r * per + j] = block[:part]
            stage[1, r * per + j] = block[part:]
        if r == order[0]:
            pl.semaphore_wait(barrier, rounds + n_col - 1)
        z_copy(0, r).start()

    def col_copy(at, d, here, send_sem, recv_sem):
        return pltpu.make_async_remote_copy(
            src_ref=at(here), dst_ref=at(here), send_sem=send_sem, recv_sem=recv_sem,
            device_id={"col": lax.rem(c + d, n_col)}, device_id_type=MESH,
        )

    load_w.wait()
    for d in range(1, n_col):
        col_copy(lambda i: w.at[i], d, c, w_send.at[d - 1], w_recv.at[d - 1]).start()
    load_cot.wait()
    for d in range(1, n_col):
        col_copy(lambda i: cot.at[i], d, c, c_send.at[d - 1], c_recv.at[d - 1]).start()

    def col_wait(at, d, send_sem, recv_sem):
        there = lax.rem(c - d + n_col, n_col)
        col_copy(at, d, c, send_sem, recv_sem).wait_send()
        col_copy(at, d, there, send_sem, recv_sem).wait_recv()

    for d in range(1, n_col):
        col_wait(lambda i: w.at[i], d, w_send.at[d - 1], w_recv.at[d - 1])
    turned = w[...].reshape(width, -1).astype(F32).T.astype(BF)
    wt[...] = turned.reshape(wt.shape)

    for r in order:
        z_copy(0, r).wait_send()
        z_copy(1, r).start()
    load_tiles.wait()

    step = blocks // CHUNKS
    span = step * size

    def agg_part(i, h):
        return lambda q: agg.at[i, q, pl.ds(h * part, part)]

    for h in range(2):
        ext = exts[h]
        for r in order:
            z_copy(h, r).wait_recv()
            if h == 1:
                z_copy(h, r).wait_send()
        for i in range(CHUNKS):
            def one(k, carry):
                b = i * step + k
                count = counts[b]
                picked = jnp.concatenate(
                    [ext[jnp.where(t < count, cols[t, b], ext_total)] for t in range(slots)], axis=1
                )
                rows = jnp.concatenate([tiles[b, t] for t in range(slots)], axis=1)
                total = nt_dot(picked, rows).astype(BF)
                columns = pl.ds(pl.multiple_of(k * size, size), size)
                agg[i, c, h * part : (h + 1) * part, columns] = total
                return carry

            lax.fori_loop(0, step, one, 0)
            for d in range(1, n_col):
                col_copy(
                    agg_part(i, h), d, c, a_send.at[h, i, d - 1], a_recv.at[h, i, d - 1]
                ).start()

    for d in range(1, n_col):
        col_wait(lambda q: cot.at[q], d, c_send.at[d - 1], c_recv.at[d - 1])

    gw = jnp.zeros((feat, width), F32)
    for i in range(CHUNKS):
        for d in range(1, n_col):
            for h in range(2):
                col_wait(agg_part(i, h), d, a_send.at[h, i, d - 1], a_recv.at[h, i, d - 1])
        whole = agg[i].reshape(width, span)
        pre = nn_dot(wt[...].reshape(width, width), whole)
        sigma = jax.nn.sigmoid(pre)
        slope = sigma * (1.0 + pre * (1.0 - sigma))
        held = cot[:, :, i * span : (i + 1) * span].reshape(width, span).astype(F32)
        grad = (held * slope).astype(BF)
        mine = nn_dot(wt[c], whole)
        out_ref[:, i * span : (i + 1) * span] = (mine * jax.nn.sigmoid(mine)).astype(BF)
        back = nn_dot(w[c], grad).astype(BF)
        for k in range(step):
            gagg_ref[i * step + k] = back[:, k * size : (k + 1) * size]
        gw = gw + nt_dot(agg[i, c], grad)
    half = gw_ref.shape[1]
    for h in range(width // half):
        gw_ref[h * feat : (h + 1) * feat] = gw[:, h * half : (h + 1) * half]


def scatter_kernel(cols, counts, gagg, tiles, own_ref, ext_ref, acc):
    step = pl.program_id(0)
    per_step, slots = tiles.shape[0], tiles.shape[1]
    blocks = own_ref.shape[0]
    total = acc.shape[0] - 1

    @pl.when(step == 0)
    def _():
        acc[...] = jnp.zeros_like(acc)

    for k in range(per_step):
        b = step * per_step + k
        count = counts[b]
        grad = gagg[k]
        for t in range(slots):
            at = jnp.where(t < count, cols[t, b], total)
            acc[at] += nn_dot(grad, tiles[k, t])

    @pl.when(step == pl.num_programs(0) - 1)
    def _():
        own_ref[...] = acc[:blocks]
        ext_ref[...] = acc[blocks:total].astype(BF)


def return_kernel(
    reduce_here, lists, ext_hbm, own, gw,
    out_ref, gw_out,
    got0, got1, got2, got3, got4, got5, got6, got7, lane_in, lane_sum, layer_in, sums,
    z_send, z_recv, a0, a1, b0, b1, c0, c1, d0, d1,
):
    sem_a, sem_b, sem_c, sem_d = (a0, a1), (b0, b1), (c0, c1), (d0, d1)
    got = [got0, got1, got2, got3, got4, got5, got6, got7]
    n_dom = lax.axis_size("dom")
    me = lax.axis_index("dom")
    rounds, per = lists.shape
    blocks, feat, size = own.shape

    def peer(distance):
        return lax.rem(me + distance + n_dom, n_dom)

    layers = n_dom // LANES
    layer = me // LANES
    lane = lax.rem(me, LANES)
    near = {round_offset(r) % n_dom for r in range(rounds)}
    if reduce_here:
        near |= {d * LANES for d in range(1, layers)}
        near |= {d % n_dom for d in range(1 - LANES, LANES) if d}
    near = sorted(near)
    barrier = pltpu.get_barrier_semaphore()
    for d in near:
        pl.semaphore_signal(barrier, inc=1, device_id={"dom": peer(d)}, device_id_type=MESH)
    for r in range(rounds):
        got[r][per] = jnp.zeros((feat, size), BF)
    pl.semaphore_wait(barrier, len(near))

    def lane_at(j):
        return lax.rem(lane + j + LANES, LANES)

    def layer_at(j):
        return lax.rem(layer + j + layers, layers)

    def dom_copy(src, dst, sems, j, target):
        return pltpu.make_async_remote_copy(
            src_ref=src, dst_ref=dst, send_sem=sems[0].at[j], recv_sem=sems[1].at[j],
            device_id={"dom": target}, device_id_type=MESH,
        )

    def lane_device(j):
        return layer * LANES + lane_at(j)

    def layer_device(j):
        return layer_at(j) * LANES + lane

    def first(j):
        return dom_copy(gw.at[lane_at(j)], lane_in.at[j], sem_a, j, lane_device(j))

    def second(j):
        return dom_copy(lane_sum.at[layer_at(j)], layer_in.at[j], sem_b, j, layer_device(j))

    def third(j, at):
        return dom_copy(sums.at[lane, at], sums.at[lane, at], sem_c, j, layer_device(j))

    def fourth(j, at):
        return dom_copy(sums.at[at], sums.at[at], sem_d, j, lane_device(j))

    def stage_one():
        for j in range(1, LANES):
            first(j).start()

    def stage_two():
        total = gw[lane]
        for j in range(1, LANES):
            first(j).wait()
            total = total + lane_in[j]
        lane_sum[...] = total
        for j in range(1, layers):
            second(j).start()

    def stage_three():
        total = lane_sum[layer]
        for j in range(1, layers):
            second(j).wait()
            total = total + layer_in[j]
        sums[lane, layer] = total
        for j in range(1, layers):
            third(j, layer).start()

    def stage_four():
        for j in range(1, layers):
            third(j, layer).wait_send()
            third(j, layer_at(-j)).wait_recv()
        for j in range(1, LANES):
            fourth(j, lane).start()

    stages = {0: stage_two, 2: stage_three, 4: stage_four} if reduce_here else {}
    if reduce_here:
        stage_one()

    copies = {}
    order = farthest_first(rounds)
    for r in order:
        copy = pltpu.make_async_remote_copy(
            src_ref=ext_hbm.at[pl.ds(r * per, per)],
            dst_ref=got[r].at[pl.ds(0, per)],
            send_sem=z_send.at[r], recv_sem=z_recv.at[r],
            device_id={"dom": peer(-round_offset(r))}, device_id_type=MESH,
        )
        copy.start()
        copies[r] = copy

    for place, r in enumerate(order):
        if place in stages:
            stages[place]()
        copies[r].wait()

        def add(b, carry):
            at = per
            for j in range(per):
                at = jnp.where(lists[r, j] == b, j, at)
            columns = pl.ds(pl.multiple_of(b * size, size), size)
            base = own[b] if place == 0 else out_ref[:, columns]
            out_ref[:, columns] = base + got[r][at].astype(F32)
            return carry

        lax.fori_loop(0, blocks, add, 0)

    if reduce_here:
        for j in range(1, LANES):
            fourth(j, lane).wait_send()
            fourth(j, lane_at(-j)).wait_recv()
        half = sums.shape[3]
        flat = sums[...].reshape(-1, half)
        feat_rows = gw_out.shape[0]
        for h in range(gw_out.shape[1] // half):
            gw_out[:, h * half : (h + 1) * half] = flat[h * feat_rows : (h + 1) * feat_rows]
    else:
        gw_out[...] = jnp.zeros_like(gw_out)


def shards(n_dom, n_col, feats_t, weight, cotangent_t, tiles, tile_cols, tile_count, send_blocks):
    feat, nodes = feats_t.shape
    width = feat * n_col
    blocks, slots, size, _ = tiles.shape
    rounds, per = send_blocks.shape[1:]
    extra = rounds * per
    lists = send_blocks[0]
    slot_cols = tile_cols.T
    step = blocks // CHUNKS
    span = step * size
    vmem = pl.BlockSpec(memory_space=pltpu.VMEM)
    smem = pl.BlockSpec(memory_space=pltpu.SMEM)
    anywhere = pl.BlockSpec(memory_space=pl.ANY)
    dma = pltpu.SemaphoreType.DMA
    half = 128

    output_t, gagg, gw = pl.pallas_call(
        forward_kernel,
        out_shape=(
            jax.ShapeDtypeStruct((feat, nodes), BF),
            jax.ShapeDtypeStruct((blocks, feat, size), BF),
            jax.ShapeDtypeStruct((feat * (width // half), half), F32),
        ),
        in_specs=[smem, smem, smem, vmem, anywhere, anywhere, anywhere],
        out_specs=(vmem, vmem, vmem),
        scratch_shapes=[
            pltpu.VMEM((blocks, feat, size), BF),
            pltpu.VMEM((2, extra, feat // 2, size), BF),
            pltpu.VMEM((blocks + extra + 1, feat // 2, size), BF),
            pltpu.VMEM((blocks + extra + 1, feat // 2, size), BF),
            pltpu.VMEM(tiles.shape, BF),
            pltpu.VMEM((n_col, feat, nodes), BF),
            pltpu.VMEM((n_col, feat, width), BF),
            pltpu.VMEM((n_col, feat, width), BF),
            pltpu.VMEM((CHUNKS, n_col, feat, span), BF),
            dma((2, rounds)), dma((2, rounds)),
            dma((n_col - 1,)), dma((n_col - 1,)),
            dma((n_col - 1,)), dma((n_col - 1,)),
            dma((2, CHUNKS, n_col - 1)), dma((2, CHUNKS, n_col - 1)),
            dma((3,)),
        ],
        compiler_params=pltpu.CompilerParams(
            collective_id=0, has_side_effects=True, vmem_limit_bytes=60 * 2**20
        ),
        name="forward",
    )(slot_cols, tile_count, lists, feats_t, cotangent_t, weight, tiles)

    per_step = blocks // CHUNKS
    own, ext = pl.pallas_call(
        scatter_kernel,
        grid=(CHUNKS,),
        out_shape=(
            jax.ShapeDtypeStruct((blocks, feat, size), F32),
            jax.ShapeDtypeStruct((extra, feat, size), BF),
        ),
        in_specs=[
            smem, smem,
            pl.BlockSpec((per_step, feat, size), lambda i: (i, 0, 0)),
            pl.BlockSpec((per_step, slots, size, size), lambda i: (i, 0, 0, 0)),
        ],
        out_specs=(
            pl.BlockSpec((blocks, feat, size), lambda i: (0, 0, 0)),
            pl.BlockSpec((extra, feat, size), lambda i: (0, 0, 0)),
        ),
        scratch_shapes=[pltpu.VMEM((blocks + extra + 1, feat, size), F32)],
        compiler_params=pltpu.CompilerParams(vmem_limit_bytes=32 * 2**20),
        name="scatter",
    )(slot_cols, tile_count, gagg, tiles)

    total_rows = feat * (width // half)
    reduce_here = n_dom % LANES == 0 and total_rows % n_dom == 0 and (total_rows // n_dom) % 8 == 0
    rows = total_rows // n_dom if reduce_here else 8
    layers = n_dom // LANES if reduce_here else 1
    gw_in = gw if reduce_here else jnp.zeros((LANES * rows, half), F32)
    gw_in = gw_in.reshape(LANES, layers, rows, half)
    grad_feats_t, grad_weight = pl.pallas_call(
        functools.partial(return_kernel, reduce_here),
        out_shape=(
            jax.ShapeDtypeStruct((feat, nodes), F32),
            jax.ShapeDtypeStruct((feat, width), F32),
        ),
        in_specs=[smem, anywhere, vmem, vmem],
        out_specs=(vmem, vmem),
        scratch_shapes=[pltpu.VMEM((per + 1, feat, size), BF)] * rounds
        + [
            pltpu.VMEM((LANES, layers, rows, half), F32),
            pltpu.VMEM((layers, rows, half), F32),
            pltpu.VMEM((layers, rows, half), F32),
            pltpu.VMEM((LANES, layers, rows, half), F32),
            dma((rounds,)), dma((rounds,)),
            dma((LANES,)), dma((LANES,)),
            dma((layers,)), dma((layers,)),
            dma((layers,)), dma((layers,)),
            dma((LANES,)), dma((LANES,)),
        ],
        compiler_params=pltpu.CompilerParams(
            collective_id=1, has_side_effects=True, vmem_limit_bytes=48 * 2**20
        ),
        name="give_back",
    )(lists, ext, own, gw_in)
    if not reduce_here:
        summed = lax.psum(gw, "dom").reshape(width // half, feat, half)
        grad_weight = summed.transpose(1, 0, 2).reshape(feat, width)
    return (output_t, grad_weight, grad_feats_t)


def solution(mesh):
    placed = (
        P("col", "dom"),
        P("col", None),
        P("col", "dom"),
        P("dom", None, None, None),
        P("dom", None),
        P("dom"),
        P("dom", None, None),
    )
    return jax.shard_map(
        functools.partial(shards, mesh.shape["dom"], mesh.shape["col"]),
        mesh=mesh,
        in_specs=placed,
        out_specs=(P("col", "dom"), P("col", None), P("col", "dom")),
        check_vma=False,
    )
```
